32 devices in a mesh: gx: 4 (over z), gy: 4 (over x, core), gz: 2 (over y).
Axes of the slice: x: 2, y: 2, z: 4, core: 2. Of those that a mesh axis runs over, the one named last changes fastest.
Arguments:
- coefficients: bfloat16 [8, 32, 32, 16, 256], P(None, 'gx', 'gy', 'gz'), may hold values from -6 to 6
- fun_count: int32 [4, 4, 2], P('gx', 'gy', 'gz'), may hold values from 64 to 256, as said below
- tile_offset: int32 [4, 4, 2], P('gx', 'gy', 'gz'), may hold values from -1 to 1
- kernel: bfloat16 [4, 256, 256], P('gx'), may hold values from -0.0234375 to 0.0234375
Outputs:
- density: float32 [4, 4, 2, 4096], P('gx', 'gy', 'gz')
The draws below stay inside these ranges and needn't reach their ends.
Inputs may be any that keep to these rules, and one draw needn't show every extreme that they name: `fun_count`: the slots below a domain's count hold its support functions; the other slots are empty. Some domain has all 256 slots live. `tile_offset`: the kernel tile of a domain is held by the first domain index that differs from its own by the offset, cyclically.
All inputs are finite; a program needn't handle non-finite values.
Results may differ from the reference program's by a relative error of at most 0.007.
Values may be sent and summed in bfloat16 or wider, within the bound.
A program may use at most 64 MiB of HBM per device.

```python
import jax
import jax.numpy as jnp
from jax import lax

CX = 8
CY = 8
CZ = 8
F = 256
DOM_X = 4
DOM_Y = 4
DOM_Z = 2
NX = 32
NY = 32
NZ = 16
CELLS = 4096


def draw_fun_count(key, part):
    counts = jax.random.randint(jax.random.fold_in(key, 11), (DOM_X * DOM_Y * DOM_Z,), F // 4, F + 1)
    chosen = jax.random.randint(jax.random.fold_in(key, 12), (), 0, DOM_X * DOM_Y * DOM_Z)
    positions = jnp.arange(DOM_X * DOM_Y * DOM_Z, dtype=jnp.int32)
    counts = jnp.where(positions == chosen, F, counts)
    return counts.reshape(DOM_X, DOM_Y, DOM_Z).astype(jnp.int32)


def plant(drawn, own_key, least, top_value):
    place = [jax.random.randint(jax.random.fold_in(own_key, axis), (), 0, length) for axis, length in enumerate(drawn.shape)]
    main_axis = drawn.shape.index(max(drawn.shape))
    beside = place[:main_axis] + [(place[main_axis] + 1) % drawn.shape[main_axis]] + place[main_axis + 1:]
    return drawn.at[tuple(place)].set(least).at[tuple(beside)].set(top_value)


def level_of(rng, shape, split, smallest, largest):
    gain = 1.0
    for dim, blocks in split:
        steps = jax.random.uniform(jax.random.fold_in(jax.random.fold_in(rng, 6), dim), (blocks,), jnp.float32, smallest / len(split), largest / len(split))
        gain = gain * jnp.repeat(jnp.exp(steps), shape[dim] // blocks).reshape((-1,) + (1,) * (len(shape) - 1 - dim))
    return gain


def bell_draw(stream_key, dims, deviation, most, cuts=(), held_as=jnp.bfloat16):
    gain = level_of(stream_key, dims, cuts, -0.22, 0.18) if cuts else 1.0
    values = jax.random.normal(stream_key, dims, jnp.float32) * deviation * gain
    return jnp.minimum(jnp.maximum(values, -most), most).astype(held_as)


def setup_inputs(seed: int = 0) -> dict:
    keys = jax.random.split(jax.random.key(seed), 5)
    coefficients = bell_draw(keys[0], (8, NX, NY, NZ, F), 1.0, 6.0, ((1, 4), (2, 4), (3, 2)))
    fun_count = draw_fun_count(jax.random.fold_in(keys[4], 71), 0)
    tile_offset = plant(jax.random.randint(keys[2], (DOM_X, DOM_Y, DOM_Z), -1, 2), jax.random.fold_in(keys[2], 1), -1, 1).astype(jnp.int32)
    kernel = bell_draw(keys[3], (DOM_X, F, F), (F * F) ** -0.5, 0.0234375, ((0, 4),))
    return {"coefficients": coefficients, "fun_count": fun_count, "tile_offset": tile_offset, "kernel": kernel}


FILT = [0.48296291314453416, 0.8365163037378079, 0.22414386804201339, -0.12940952255126037]
WAVE = [(1.0 if t % 2 == 0 else -1.0) * FILT[3 - t] for t in range(4)]


def band_table(coarse):
    fine_idx = jnp.arange(2 * coarse, dtype=jnp.int32)[:, None]
    coarse_idx = jnp.arange(coarse + 2, dtype=jnp.int32)[None, :]
    offset = fine_idx - 2 * coarse_idx + 3
    low = jnp.zeros(offset.shape, jnp.float32)
    high = jnp.zeros(offset.shape, jnp.float32)
    for tap in range(4):
        low = low + jnp.where(offset == tap, FILT[tap], 0.0).astype(jnp.float32)
        high = high + jnp.where(offset == tap, WAVE[tap], 0.0).astype(jnp.float32)
    return jnp.stack([low, high])


def synthesize(box, table_x, table_y, table_z):
    high = lax.Precision.HIGHEST
    data = box.astype(jnp.float32)
    data = data.reshape((2, 4) + data.shape[1:])
    after_x = jnp.einsum("cnk,cpkyzf->pnyzf", table_x, data, precision=high).astype(jnp.bfloat16)
    data = after_x.astype(jnp.float32)
    data = data.reshape((2, 2) + data.shape[1:])
    after_y = jnp.einsum("cnk,cpxkzf->pxnzf", table_y, data, precision=high).astype(jnp.bfloat16)
    data = after_y.astype(jnp.float32)
    return jnp.einsum("cnk,cxykf->xynf", table_z, data, precision=high).astype(jnp.bfloat16)


def reference(coefficients, fun_count, tile_offset, kernel):
    live_count = jnp.repeat(jnp.repeat(jnp.repeat(fun_count, CX, axis=0), CY, axis=1), CZ, axis=2)
    slots = jnp.arange(F, dtype=jnp.int32)
    mask = slots[None, None, None, :] < live_count[:, :, :, None]
    live = jnp.where(mask[None], coefficients, jnp.zeros((), jnp.bfloat16))
    padded = jnp.pad(live, ((0, 0), (1, 1), (1, 1), (1, 1), (0, 0)))
    table_x = band_table(CX)
    table_y = band_table(CY)
    table_z = band_table(CZ)

    def one_domain(index):
        dom_x = index // (DOM_Y * DOM_Z)
        dom_y = (index // DOM_Z) % DOM_Y
        dom_z = index % DOM_Z
        zero = jnp.zeros((), jnp.int32)
        box = lax.dynamic_slice(padded, (zero, (dom_x * CX).astype(jnp.int32), (dom_y * CY).astype(jnp.int32), (dom_z * CZ).astype(jnp.int32), zero), (8, CX + 2, CY + 2, CZ + 2, F))
        phi = synthesize(box, table_x, table_y, table_z).reshape(CELLS, F)
        owner = ((dom_x + tile_offset[dom_x, dom_y, dom_z]) % DOM_X).astype(jnp.int32)
        tile = lax.dynamic_index_in_dim(kernel, owner, 0, keepdims=False)
        psi = jnp.dot(phi, tile, preferred_element_type=jnp.float32)
        return jnp.sum(phi.astype(jnp.float32) * psi, axis=1)

    density = lax.map(one_domain, jnp.arange(DOM_X * DOM_Y * DOM_Z, dtype=jnp.int32))
    return density.reshape(DOM_X, DOM_Y, DOM_Z, CELLS)
```

```python
import jax
import jax.numpy as jnp
import numpy as np
from jax import lax
from jax.experimental import pallas as pl
from jax.experimental.pallas import tpu as pltpu
from jax.sharding import PartitionSpec as P

FILT = [0.48296291314453416, 0.8365163037378079, 0.2241438680420134, -0.12940952255126037]
WAVE = [(1.0 if t % 2 == 0 else -1.0) * FILT[3 - t] for t in range(4)]
BANDS = (FILT, WAVE)
MESH = pl.DeviceIdType.MESH
BF = jnp.bfloat16
F32 = jnp.float32


def synthesis(coarse):
    table = np.zeros((2 * coarse, 2, coarse))
    for n in range(2 * coarse):
        for k in range(coarse):
            t = n - 2 * k + 1
            if 0 <= t < 4:
                for b in range(2):
                    table[n, b, k] = BANDS[b][t]
    return table


def best_scale():
    taps = np.array(FILT)
    prods = (taps[:, None] * taps[None, :]).reshape(-1)
    scales = np.linspace(1.0, 2.0, 4001)
    scaled = scales[:, None] * prods[None, :]
    rounded = scaled.astype(jnp.bfloat16).astype(np.float64)
    errors = np.sum(((rounded - scaled) / scales[:, None]) ** 2, axis=1)
    return float(scales[int(np.argmin(errors))])


def tables(cy, cz, scale):
    sy, sz = synthesis(cy), synthesis(cz)
    ny, nz = 2 * cy, 2 * cz
    rows = 4 * cy * cz
    own = np.einsum("ybk,zcl->zybckl", sy, sz).reshape(ny * nz, rows)
    halo = np.zeros((nz, ny, 2, 2, cz))
    halo[:, 0, 0] = sz
    halo[:, ny - 1, 1] = sz
    send_y = np.zeros((2, 2, cz, 2, 2, cy, cz))
    send_z = np.zeros((2, ny, 2, 2, cy, cz))
    send_zh = np.zeros((2, ny, 2, 2, cz))
    for b in range(2):
        for c in range(2):
            for l in range(cz):
                send_y[0, c, l, b, c, cy - 1, l] = BANDS[b][3]
                send_y[1, c, l, b, c, 0, l] = BANDS[b][0]
            send_z[0, :, b, c, :, cz - 1] = sy[:, b] * BANDS[c][3]
            send_z[1, :, b, c, :, 0] = sy[:, b] * BANDS[c][0]
    for c in range(2):
        for side, row in ((0, 0), (1, ny - 1)):
            send_zh[0, row, side, c, cz - 1] = BANDS[c][3]
            send_zh[1, row, side, c, 0] = BANDS[c][0]
    wide = lambda a, r: a.reshape(r, -1)
    main = np.concatenate([scale * own, wide(send_y, 4 * cz), scale * wide(send_z, 2 * ny)], 0)
    small = np.concatenate([wide(halo, ny * nz), wide(send_zh, 2 * ny)], 0) * scale
    return main.astype(jnp.bfloat16), small.astype(jnp.bfloat16)


def rowsum(prod):
    width = prod.shape[1] // 2
    half = prod[:, :width] + prod[:, width:]
    return jnp.sum(half.T, axis=0, keepdims=True)


def make_kernel(cx, cy, cz, slots, scale):
    fx, fy, fz = 2 * cx, 2 * cy, 2 * cz
    face = cy * cz
    cells = fy * fz
    rows = 4 * face
    inv = 1.0 / (scale * scale)

    def kernel(coef, cnt, off, ktile, main_h, small_h, den, denb,
               cv, ax, main, small, xo, xi, yo, yi, zo, zi, zb, tiles, tile, lsem, ssem, rsem):
        ix, iy, iz = lax.axis_index("gx"), lax.axis_index("gy"), lax.axis_index("gz")
        gx, gy, gz = lax.axis_size("gx"), lax.axis_size("gy"), lax.axis_size("gz")
        index = {"gx": ix, "gy": iy, "gz": iz}
        size = {"gx": gx, "gy": gy, "gz": gz}

        def local(i, src, dst):
            return pltpu.make_async_copy(src, dst, lsem.at[i])

        loads = [
            local(0, coef.at[:, 0], cv.at[:, 0]),
            local(1, coef.at[:, cx - 1], cv.at[:, cx - 1]),
            local(2, coef.at[:, pl.ds(1, cx - 2)], cv.at[:, pl.ds(1, cx - 2)]),
            local(3, main_h, main),
            local(4, small_h, small),
            local(5, ktile.at[0], tiles.at[2]),
        ]
        for load in loads:
            load.start()

        def has(axis, step):
            return index[axis] < size[axis] - 1 if step > 0 else index[axis] > 0

        barrier = pltpu.get_barrier_semaphore()
        ring = {1: lax.rem(ix + 1, gx), -1: lax.rem(ix + gx - 1, gx)}
        for step in (1, -1):
            pl.semaphore_signal(barrier, inc=1, device_id={"gx": ring[step]}, device_id_type=MESH)
            for axis in ("gy", "gz"):
                @pl.when(has(axis, step))
                def _():
                    pl.semaphore_signal(
                        barrier, inc=1, device_id={axis: index[axis] + step}, device_id_type=MESH
                    )

        def remote(i, src, dst, axis, target):
            return pltpu.make_async_remote_copy(
                src_ref=src, dst_ref=dst, send_sem=ssem.at[i], recv_sem=rsem.at[i],
                device_id={axis: target}, device_id_type=MESH,
            )

        early, late = pl.ds(2, fx - 2), pl.ds(0, 2)
        up, dn = 0, 1
        copies = {}
        for side, step in ((up, 1), (dn, -1)):
            copies["x", side] = (remote(side, xo.at[side], xi.at[side], "gx", ix + step), "gx", step)
            for part, (name, planes) in enumerate((("e", early), ("l", late))):
                copies["y" + name, side] = (
                    remote(4 + 2 * part + side, yo.at[side, planes],
                           yi.at[planes, pl.ds(side * 2 * cz, 2 * cz)], "gy", iy + step),
                    "gy", step)
                copies["z" + name, side] = (
                    remote(8 + 2 * part + side, zo.at[side, planes], zi.at[side, planes], "gz", iz + step),
                    "gz", step)
        rings = [remote(2 + side, ktile.at[0], tiles.at[side], "gx", ring[step])
                 for side, step in ((up, 1), (dn, -1))]

        def start(key):
            copy, axis, step = copies[key]
            pl.when(has(axis, step))(lambda: copy.start())

        def arrive(key):
            copy, axis, step = copies[key]
            pl.when(has(axis, -step))(lambda: copy.wait_recv())

        @pl.when(ix == 0)
        def _():
            xi[0] = jnp.zeros(xi.shape[1:], BF)

        @pl.when(ix == gx - 1)
        def _():
            xi[1] = jnp.zeros(xi.shape[1:], BF)

        @pl.when(iy == 0)
        def _():
            yi[:, 0 : 2 * cz] = jnp.zeros((fx, 2 * cz, slots), BF)

        @pl.when(iy == gy - 1)
        def _():
            yi[:, 2 * cz : 4 * cz] = jnp.zeros((fx, 2 * cz, slots), BF)

        @pl.when(iz == 0)
        def _():
            zi[0] = jnp.zeros(zi.shape[1:], BF)

        @pl.when(iz == gz - 1)
        def _():
            zi[1] = jnp.zeros(zi.shape[1:], BF)

        live = jnp.where(
            lax.broadcasted_iota(jnp.int32, (1, slots), 1) < cnt[0, 0, 0], 1.0, 0.0
        ).astype(F32)
        low = [FILT[t] * live for t in range(4)]
        high = [WAVE[t] * live for t in range(4)]

        def bands(k, p):
            return cv[p, k].astype(F32), cv[4 + p, k].astype(F32)

        def block(p):
            return pl.ds(p * face, face)

        loads[0].wait()
        for p in range(4):
            s, w = bands(0, p)
            xo[dn, block(p)] = (low[0] * s + high[0] * w).astype(BF)
        loads[1].wait()
        for p in range(4):
            s, w = bands(cx - 1, p)
            xo[up, block(p)] = (low[3] * s + high[3] * w).astype(BF)
        peers = 2
        for axis in ("gy", "gz"):
            i, n = index[axis], size[axis]
            peers = peers + (i + n - 1) // n + ((i + 1) % n + n - 1) // n
        pl.semaphore_wait(barrier, peers)
        start(("x", dn))
        start(("x", up))
        for copy in rings:
            copy.start()

        loads[2].wait()

        @pl.loop(1, cx)
        def _(m):
            for p in range(4):
                s0, w0 = bands(m - 1, p)
                s1, w1 = bands(m, p)
                ax[2 * m, block(p)] = (
                    low[2] * s0 + high[2] * w0 + low[0] * s1 + high[0] * w1
                ).astype(BF)
                ax[2 * m + 1, block(p)] = (
                    low[1] * s1 + high[1] * w1 + low[3] * s0 + high[3] * w0
                ).astype(BF)

        loads[3].wait()
        half = 2 * cz

        def send_y(q):
            out = jnp.dot(main[pl.ds(cells, 2 * half), :], ax[q], preferred_element_type=F32)
            yo[up, q] = out[:half].astype(BF)
            yo[dn, q] = out[half:].astype(BF)

        pl.loop(2, fx)(send_y)
        start(("ye", up))
        start(("ye", dn))

        arrive(("x", up))
        arrive(("x", dn))
        for p in range(4):
            s, w = bands(cx - 1, p)
            ax[0, block(p)] = (low[2] * s + high[2] * w + xi[dn, block(p)].astype(F32)).astype(BF)
            s, w = bands(0, p)
            ax[1, block(p)] = (low[1] * s + high[1] * w + xi[up, block(p)].astype(F32)).astype(BF)
        pl.loop(0, 2)(send_y)
        start(("yl", up))
        start(("yl", dn))

        loads[4].wait()

        def send_z(q):
            out = jnp.dot(main[pl.ds(cells + 2 * half, 2 * fy), :], ax[q], preferred_element_type=F32)
            out += jnp.dot(small[pl.ds(cells, 2 * fy), :], yi[q], preferred_element_type=F32)
            zo[up, q] = out[:fy].astype(BF)
            zo[dn, q] = out[fy:].astype(BF)

        arrive(("ye", up))
        arrive(("ye", dn))
        pl.loop(2, fx)(send_z)
        start(("ze", up))
        start(("ze", dn))
        arrive(("yl", up))
        arrive(("yl", dn))
        pl.loop(0, 2)(send_z)
        start(("zl", up))
        start(("zl", dn))

        loads[5].wait()
        for copy in rings:
            copy.wait_recv()
        away = off[0, 0, 0]
        before = jnp.where(away == -1, 1.0, 0.0).astype(F32)
        after = jnp.where(away == 1, 1.0, 0.0).astype(F32)
        here = 1.0 - before - after
        tile[...] = (
            tiles[up].astype(F32) * before + tiles[dn].astype(F32) * after
            + tiles[2].astype(F32) * here
        ).astype(BF)

        @pl.loop(0, fx)
        def _(q):
            pre = jnp.dot(main[pl.ds(0, cells), :], ax[q], preferred_element_type=F32)
            pre += jnp.dot(small[pl.ds(0, cells), :], yi[q], preferred_element_type=F32)
            zb[0, q] = pre[:fy]
            zb[1, q] = pre[cells - fy :]
            phi = pre.astype(BF)
            psi = jnp.dot(phi, tile[...], preferred_element_type=F32)
            den[pl.ds(q, 1), :] = rowsum(phi.astype(F32) * psi) * inv

        for key in (("ze", up), ("ze", dn), ("zl", up), ("zl", dn)):
            arrive(key)
        for side in range(2):
            pre = zb[side] + zi[side].astype(F32)
            phi = pre.reshape(fx * fy, slots).astype(BF)
            psi = jnp.dot(phi, tile[...], preferred_element_type=F32)
            denb[pl.ds(side, 1), :] = rowsum(phi.astype(F32) * psi) * inv

        for copy, axis, step in copies.values():
            pl.when(has(axis, step))(lambda copy=copy: copy.wait_send())
        for copy in rings:
            copy.wait_send()

    return kernel


def body(coefficients, fun_count, tile_offset, kernel):
    bands, cx, cy, cz, slots = coefficients.shape
    fx, fy, fz = 2 * cx, 2 * cy, 2 * cz
    cells, rows = fy * fz, 4 * cy * cz
    scale = best_scale()
    main, small = tables(cy, cz, scale)
    anywhere = pl.BlockSpec(memory_space=pl.ANY)
    scalar = pl.BlockSpec(memory_space=pltpu.SMEM)
    vmem = pl.BlockSpec(memory_space=pltpu.VMEM)
    den, denb = pl.pallas_call(
        make_kernel(cx, cy, cz, slots, scale),
        out_shape=(
            jax.ShapeDtypeStruct((fx, cells), F32),
            jax.ShapeDtypeStruct((2, fx * fy), F32),
        ),
        in_specs=[anywhere, scalar, scalar, anywhere, anywhere, anywhere],
        out_specs=(vmem, vmem),
        scratch_shapes=[
            pltpu.VMEM((bands, cx, cy * cz, slots), BF),
            pltpu.VMEM((fx, rows, slots), BF),
            pltpu.VMEM(main.shape, BF),
            pltpu.VMEM(small.shape, BF),
            pltpu.VMEM((2, rows, slots), BF),
            pltpu.VMEM((2, rows, slots), BF),
            pltpu.VMEM((2, fx, 2 * cz, slots), BF),
            pltpu.VMEM((fx, 4 * cz, slots), BF),
            pltpu.VMEM((2, fx, fy, slots), BF),
            pltpu.VMEM((2, fx, fy, slots), BF),
            pltpu.VMEM((2, fx, fy, slots), F32),
            pltpu.VMEM((3, slots, slots), BF),
            pltpu.VMEM((slots, slots), BF),
            pltpu.SemaphoreType.DMA((6,)),
            pltpu.SemaphoreType.DMA((12,)),
            pltpu.SemaphoreType.DMA((12,)),
        ],
        compiler_params=pltpu.CompilerParams(
            collective_id=0, has_side_effects=True, vmem_limit_bytes=40 * 2**20
        ),
    )(
        coefficients.reshape(bands, cx, cy * cz, slots),
        fun_count, tile_offset, kernel, jnp.asarray(main), jnp.asarray(small),
    )
    den = jnp.roll(den, -1, axis=0).reshape(fx, fz, fy)
    faces = jnp.roll(denb.reshape(2, fx, fy), -1, axis=1)
    den = jnp.concatenate([faces[0][:, None], den[:, 1:-1], faces[1][:, None]], axis=1)
    return den.transpose(0, 2, 1).reshape(1, 1, 1, -1)


def solution(mesh):
    placed = (
        P(None, "gx", "gy", "gz", None),
        P("gx", "gy", "gz"),
        P("gx", "gy", "gz"),
        P("gx", None, None),
    )
    return jax.shard_map(
        body, mesh=mesh, in_specs=placed, out_specs=P("gx", "gy", "gz", None), check_vma=False
    )
```

```python
import jax
import jax.numpy as jnp
import numpy as np
from jax import lax
from jax.experimental import pallas as pl
from jax.experimental.pallas import tpu as pltpu
from jax.sharding import PartitionSpec as P

FILT = [0.48296291314453416, 0.8365163037378079, 0.2241438680420134, -0.12940952255126037]
WAVE = [(1.0 if t % 2 == 0 else -1.0) * FILT[3 - t] for t in range(4)]
BANDS = (FILT, WAVE)
MESH = pl.DeviceIdType.MESH
BF = jnp.bfloat16
F32 = jnp.float32


def synthesis(coarse):
    table = np.zeros((2 * coarse, 2, coarse))
    for n in range(2 * coarse):
        for k in range(coarse):
            t = n - 2 * k + 1
            if 0 <= t < 4:
                for b in range(2):
                    table[n, b, k] = BANDS[b][t]
    return table


def best_scale():
    taps = np.array(FILT)
    prods = (taps[:, None] * taps[None, :]).reshape(-1)
    scales = np.linspace(1.0, 2.0, 4001)
    scaled = scales[:, None] * prods[None, :]
    rounded = scaled.astype(jnp.bfloat16).astype(np.float64)
    errors = np.sum(((rounded - scaled) / scales[:, None]) ** 2, axis=1)
    return float(scales[int(np.argmin(errors))])


def cell_order(fy, fz):
    z_faces = [(z, y) for z in (0, fz - 1) for y in range(fy)]
    y_faces = [(z, y) for y in (0, fy - 1) for z in range(1, fz - 1)]
    inner = [(z, y) for z in range(1, fz - 1) for y in range(1, fy - 1)]
    fill = -len(y_faces) % 16
    y_faces, inner = y_faces + inner[:fill], inner[fill:]
    return inner + y_faces + z_faces, len(inner), len(y_faces), len(z_faces)


def tables(cy, cz, scale):
    sy, sz = synthesis(cy), synthesis(cz)
    fy, fz = 2 * cy, 2 * cz
    rows = 4 * cy * cz
    order, inner, y_rows, z_rows = cell_order(fy, fz)
    pick = np.array([z * fy + y for z, y in order])
    own = np.einsum("ybk,zcl->zybckl", sy, sz).reshape(fy * fz, rows)[pick]
    halo = np.zeros((fz, fy, 2, 2, cz))
    halo[:, 0, 0] = sz
    halo[:, fy - 1, 1] = sz
    halo = halo.reshape(fy * fz, 4 * cz)[pick]
    send_z = np.zeros((2, fy, 2, 2, cy, cz))
    send_zh = np.zeros((2, fy, 2, 2, cz))
    for c in range(2):
        for b in range(2):
            send_z[0, :, b, c, :, cz - 1] = sy[:, b] * BANDS[c][3]
            send_z[1, :, b, c, :, 0] = sy[:, b] * BANDS[c][0]
        for side, row in ((0, 0), (1, fy - 1)):
            send_zh[0, row, side, c, cz - 1] = BANDS[c][3]
            send_zh[1, row, side, c, 0] = BANDS[c][0]
    main = scale * np.concatenate([own, send_z.reshape(2 * fy, rows)], 0)
    small = scale * np.concatenate([halo[inner:], send_zh.reshape(2 * fy, 4 * cz)], 0)
    back = np.zeros((fy * fz, fy * fz))
    for at, (z, y) in enumerate(order):
        back[at, y * fz + z] = 1.0
    return [t.astype(jnp.bfloat16) for t in (main, small, back)]


def rowsum(prod):
    width = prod.shape[1] // 2
    half = prod[:, :width] + prod[:, width:]
    return jnp.sum(half.T, axis=0, keepdims=True)


def make_kernel(cx, cy, cz, slots, scale):
    fx, fy, fz = 2 * cx, 2 * cy, 2 * cz
    face = cy * cz
    cells = fy * fz
    rows = 4 * face
    inv = 1.0 / (scale * scale)
    _, inner, y_rows, z_rows = cell_order(fy, fz)
    edge = y_rows + z_rows

    def kernel(coef, cnt, off, ktile, main_h, small_h, back_h, den,
               cv, ax, main, small, back, xo, xi, yo, yi, zo, zi, phis, edges, den_in, den_ed,
               tiles, tile, lsem, ssem, rsem):
        ix, iy, iz = lax.axis_index("gx"), lax.axis_index("gy"), lax.axis_index("gz")
        gx, gy, gz = lax.axis_size("gx"), lax.axis_size("gy"), lax.axis_size("gz")
        index = {"gx": ix, "gy": iy, "gz": iz}
        size = {"gx": gx, "gy": gy, "gz": gz}

        def local(i, src, dst):
            return pltpu.make_async_copy(src, dst, lsem.at[i])

        loads = [
            local(0, coef.at[:, 0], cv.at[:, 0]),
            local(1, coef.at[:, cx - 1], cv.at[:, cx - 1]),
            local(2, coef.at[:, pl.ds(1, cx - 2)], cv.at[:, pl.ds(1, cx - 2)]),
            local(3, main_h, main),
            local(4, small_h, small),
            local(5, ktile.at[0], tiles.at[2]),
            local(6, back_h, back),
        ]
        for load in loads:
            load.start()

        def has(axis, step):
            return index[axis] < size[axis] - 1 if step > 0 else index[axis] > 0

        barrier = pltpu.get_barrier_semaphore()
        ring = {1: lax.rem(ix + 1, gx), -1: lax.rem(ix + gx - 1, gx)}
        for step in (1, -1):
            pl.semaphore_signal(barrier, inc=1, device_id={"gx": ring[step]}, device_id_type=MESH)
            for axis in ("gy", "gz"):
                @pl.when(has(axis, step))
                def _():
                    pl.semaphore_signal(
                        barrier, inc=1, device_id={axis: index[axis] + step}, device_id_type=MESH
                    )

        def remote(i, src, dst, axis, target):
            return pltpu.make_async_remote_copy(
                src_ref=src, dst_ref=dst, send_sem=ssem.at[i], recv_sem=rsem.at[i],
                device_id={axis: target}, device_id_type=MESH,
            )

        early, late = pl.ds(2, fx - 2), pl.ds(0, 2)
        up, dn = 0, 1
        copies = {}
        for side, step in ((up, 1), (dn, -1)):
            copies["x", side] = (remote(side, xo.at[side], xi.at[side], "gx", ix + step), "gx", step)
            for part, (name, planes) in enumerate((("e", early), ("l", late))):
                copies["y" + name, side] = (
                    remote(4 + 2 * part + side, yo.at[side, planes],
                           yi.at[planes, pl.ds(side * 2 * cz, 2 * cz)], "gy", iy + step),
                    "gy", step)
                copies["z" + name, side] = (
                    remote(8 + 2 * part + side, zo.at[side, planes], zi.at[side, planes], "gz", iz + step),
                    "gz", step)
        rings = [remote(2 + side, ktile.at[0], tiles.at[side], "gx", ring[step])
                 for side, step in ((up, 1), (dn, -1))]

        def start(key):
            copy, axis, step = copies[key]
            pl.when(has(axis, step))(lambda: copy.start())

        def arrive(key):
            copy, axis, step = copies[key]
            pl.when(has(axis, -step))(lambda: copy.wait_recv())

        @pl.when(ix == 0)
        def _():
            xi[0] = jnp.zeros(xi.shape[1:], BF)

        @pl.when(ix == gx - 1)
        def _():
            xi[1] = jnp.zeros(xi.shape[1:], BF)

        @pl.when(iy == 0)
        def _():
            yi[:, 0 : 2 * cz] = jnp.zeros((fx, 2 * cz, slots), BF)

        @pl.when(iy == gy - 1)
        def _():
            yi[:, 2 * cz : 4 * cz] = jnp.zeros((fx, 2 * cz, slots), BF)

        @pl.when(iz == 0)
        def _():
            zi[0] = jnp.zeros(zi.shape[1:], BF)

        @pl.when(iz == gz - 1)
        def _():
            zi[1] = jnp.zeros(zi.shape[1:], BF)

        live = jnp.where(
            lax.broadcasted_iota(jnp.int32, (1, slots), 1) < cnt[0, 0, 0], 1.0, 0.0
        ).astype(F32)
        low = [FILT[t] * live for t in range(4)]
        high = [WAVE[t] * live for t in range(4)]

        def bands(k, p):
            return cv[p, k].astype(F32), cv[4 + p, k].astype(F32)

        def block(p):
            return pl.ds(p * face, face)

        loads[0].wait()
        for p in range(4):
            s, w = bands(0, p)
            xo[dn, block(p)] = (low[0] * s + high[0] * w).astype(BF)
        loads[1].wait()
        for p in range(4):
            s, w = bands(cx - 1, p)
            xo[up, block(p)] = (low[3] * s + high[3] * w).astype(BF)
        peers = 2
        for axis in ("gy", "gz"):
            i, n = index[axis], size[axis]
            peers = peers + (i + n - 1) // n + ((i + 1) % n + n - 1) // n
        pl.semaphore_wait(barrier, peers)
        start(("x", dn))
        start(("x", up))
        for copy in rings:
            copy.start()

        loads[2].wait()

        def send_y(q):
            for side, tap, k in ((up, 3, cy - 1), (dn, 0, 0)):
                parts = []
                for c in range(2):
                    s = ax[q, pl.ds(c * face + k * cz, cz)].astype(F32)
                    w = ax[q, pl.ds((2 + c) * face + k * cz, cz)].astype(F32)
                    parts.append(FILT[tap] * s + WAVE[tap] * w)
                yo[side, q] = jnp.concatenate(parts, axis=0).astype(BF)

        @pl.loop(1, cx)
        def _(m):
            for p in range(4):
                s0, w0 = bands(m - 1, p)
                s1, w1 = bands(m, p)
                ax[2 * m, block(p)] = (
                    low[2] * s0 + high[2] * w0 + low[0] * s1 + high[0] * w1
                ).astype(BF)
                ax[2 * m + 1, block(p)] = (
                    low[1] * s1 + high[1] * w1 + low[3] * s0 + high[3] * w0
                ).astype(BF)
            send_y(2 * m)
            send_y(2 * m + 1)

        start(("ye", up))
        start(("ye", dn))
        loads[3].wait()
        loads[4].wait()

        def own_cells(q):
            pre = jnp.dot(main[...], ax[q], preferred_element_type=F32)
            phis[q] = pre[:inner].astype(BF)
            edges[q] = pre[inner:]

        for q in range(2, fx):
            own_cells(q)

        arrive(("x", up))
        arrive(("x", dn))
        for p in range(4):
            s, w = bands(cx - 1, p)
            ax[0, block(p)] = (low[2] * s + high[2] * w + xi[dn, block(p)].astype(F32)).astype(BF)
            s, w = bands(0, p)
            ax[1, block(p)] = (low[1] * s + high[1] * w + xi[up, block(p)].astype(F32)).astype(BF)
        send_y(0)
        send_y(1)
        start(("yl", up))
        start(("yl", dn))

        def y_halo(q):
            pre = edges[q] + jnp.dot(small[...], yi[q], preferred_element_type=F32)
            edges[q, :edge] = pre[:edge]
            zo[up, q] = pre[edge : edge + fy].astype(BF)
            zo[dn, q] = pre[edge + fy :].astype(BF)

        arrive(("ye", up))
        arrive(("ye", dn))
        for q in range(2, fx):
            y_halo(q)
        start(("ze", up))
        start(("ze", dn))
        own_cells(0)
        own_cells(1)
        arrive(("yl", up))
        arrive(("yl", dn))
        y_halo(0)
        y_halo(1)
        start(("zl", up))
        start(("zl", dn))

        loads[5].wait()
        loads[6].wait()
        for copy in rings:
            copy.wait_recv()
        away = off[0, 0, 0]
        before = jnp.where(away == -1, 1.0, 0.0).astype(F32)
        after = jnp.where(away == 1, 1.0, 0.0).astype(F32)
        here = 1.0 - before - after
        tile[...] = (
            tiles[up].astype(F32) * before + tiles[dn].astype(F32) * after
            + tiles[2].astype(F32) * here
        ).astype(BF)

        def dens(phi):
            psi = jnp.dot(phi, tile[...], preferred_element_type=F32)
            return rowsum(phi.astype(F32) * psi) * inv

        for q in range(fx):
            den_in[pl.ds((q - 1) % fx, 1), :] = dens(phis[q])

        def edge_cells(pre, at, width):
            row = dens(pre.reshape(fx * width, slots).astype(BF))
            for q in range(fx):
                den_ed[pl.ds((q - 1) % fx, 1), pl.ds(at, width)] = row[:, q * width : (q + 1) * width]

        def restore(value, at):
            return jnp.dot(value, back[pl.ds(at, value.shape[1]), :].astype(F32),
                           precision=lax.Precision.HIGHEST, preferred_element_type=F32)

        edge_cells(edges[:, :y_rows], 0, y_rows)
        placed = restore(den_in[...], 0)
        for key in (("ze", up), ("ze", dn), ("zl", up), ("zl", dn)):
            arrive(key)
        pre = jnp.concatenate([
            edges[:, y_rows : y_rows + fy] + zi[0].astype(F32),
            edges[:, y_rows + fy : edge] + zi[1].astype(F32),
        ], axis=1)
        edge_cells(pre, y_rows, z_rows)
        den[...] = placed + restore(den_ed[...], inner)

        for copy, axis, step in copies.values():
            pl.when(has(axis, step))(lambda copy=copy: copy.wait_send())
        for copy in rings:
            copy.wait_send()

    return kernel


def body(coefficients, fun_count, tile_offset, kernel):
    bands, cx, cy, cz, slots = coefficients.shape
    fx, fy, fz = 2 * cx, 2 * cy, 2 * cz
    cells, rows = fy * fz, 4 * cy * cz
    scale = best_scale()
    main, small, back = tables(cy, cz, scale)
    _, inner, y_rows, z_rows = cell_order(fy, fz)
    anywhere = pl.BlockSpec(memory_space=pltpu.HBM)
    scalar = pl.BlockSpec(memory_space=pltpu.SMEM)
    vmem = pl.BlockSpec(memory_space=pltpu.VMEM)
    den = pl.pallas_call(
        make_kernel(cx, cy, cz, slots, scale),
        out_shape=jax.ShapeDtypeStruct((fx, cells), F32),
        in_specs=[anywhere, scalar, scalar, anywhere, anywhere, anywhere, anywhere],
        out_specs=vmem,
        scratch_shapes=[
            pltpu.VMEM((bands, cx, cy * cz, slots), BF),
            pltpu.VMEM((fx, rows, slots), BF),
            pltpu.VMEM(main.shape, BF),
            pltpu.VMEM(small.shape, BF),
            pltpu.VMEM(back.shape, BF),
            pltpu.VMEM((2, rows, slots), BF),
            pltpu.VMEM((2, rows, slots), BF),
            pltpu.VMEM((2, fx, 2 * cz, slots), BF),
            pltpu.VMEM((fx, 4 * cz, slots), BF),
            pltpu.VMEM((2, fx, fy, slots), BF),
            pltpu.VMEM((2, fx, fy, slots), BF),
            pltpu.VMEM((fx, inner, slots), BF),
            pltpu.VMEM((fx, main.shape[0] - inner, slots), F32),
            pltpu.VMEM((fx, inner), F32),
            pltpu.VMEM((fx, y_rows + z_rows), F32),
            pltpu.VMEM((3, slots, slots), BF),
            pltpu.VMEM((slots, slots), BF),
            pltpu.SemaphoreType.DMA((7,)),
            pltpu.SemaphoreType.DMA((12,)),
            pltpu.SemaphoreType.DMA((12,)),
        ],
        compiler_params=pltpu.CompilerParams(
            collective_id=0, has_side_effects=True, vmem_limit_bytes=63 * 2**20
        ),
    )(
        coefficients.reshape(bands, cx, cy * cz, slots),
        fun_count, tile_offset, kernel, jnp.asarray(main), jnp.asarray(small),
        jnp.asarray(back),
    )
    return den.reshape(1, 1, 1, -1)


def solution(mesh):
    placed = (
        P(None, "gx", "gy", "gz", None),
        P("gx", "gy", "gz"),
        P("gx", "gy", "gz"),
        P("gx", None, None),
    )
    return jax.shard_map(
        body, mesh=mesh, in_specs=placed, out_specs=P("gx", "gy", "gz", None), check_vma=False
    )
```

```python
import jax
import jax.numpy as jnp
import numpy as np
from jax import lax
from jax.experimental import pallas as pl
from jax.experimental.pallas import tpu as pltpu
from jax.sharding import PartitionSpec as P

FILT = [0.48296291314453416, 0.8365163037378079, 0.2241438680420134, -0.12940952255126037]
WAVE = [(1.0 if t % 2 == 0 else -1.0) * FILT[3 - t] for t in range(4)]
BANDS = (FILT, WAVE)
MESH = pl.DeviceIdType.MESH
BF = jnp.bfloat16
F32 = jnp.float32


def synthesis(coarse):
    table = np.zeros((2 * coarse, 2, coarse))
    for n in range(2 * coarse):
        for k in range(coarse):
            t = n - 2 * k + 1
            if 0 <= t < 4:
                for b in range(2):
                    table[n, b, k] = BANDS[b][t]
    return table


def best_scale():
    taps = np.array(FILT)
    prods = (taps[:, None] * taps[None, :]).reshape(-1)
    scales = np.linspace(1.0, 2.0, 4001)
    scaled = scales[:, None] * prods[None, :]
    rounded = scaled.astype(jnp.bfloat16).astype(np.float64)
    errors = np.sum(((rounded - scaled) / scales[:, None]) ** 2, axis=1)
    return float(scales[int(np.argmin(errors))])


def cell_order(fy, fz):
    z_faces = [(z, y) for z in (0, fz - 1) for y in range(fy)]
    y_faces = [(z, y) for y in (0, fy - 1) for z in range(1, fz - 1)]
    inner = [(z, y) for z in range(1, fz - 1) for y in range(1, fy - 1)]
    fill = -len(y_faces) % 16
    y_faces, inner = y_faces + inner[:fill], inner[fill:]
    return inner + y_faces + z_faces, len(inner), len(y_faces), len(z_faces)


def tables(cy, cz, scale):
    sy, sz = synthesis(cy), synthesis(cz)
    fy, fz = 2 * cy, 2 * cz
    rows = 4 * cy * cz
    order, inner, y_rows, z_rows = cell_order(fy, fz)
    pick = np.array([z * fy + y for z, y in order])
    own = np.einsum("ybk,zcl->zybckl", sy, sz).reshape(fy * fz, rows)[pick]
    halo = np.zeros((fz, fy, 2, 2, cz))
    halo[:, 0, 0] = sz
    halo[:, fy - 1, 1] = sz
    halo = halo.reshape(fy * fz, 4 * cz)[pick]
    send_z = np.zeros((2, fy, 2, 2, cy, cz))
    send_zh = np.zeros((2, 2, 2, 2, cz))
    for c in range(2):
        for b in range(2):
            send_z[0, :, b, c, :, cz - 1] = sy[:, b] * BANDS[c][3]
            send_z[1, :, b, c, :, 0] = sy[:, b] * BANDS[c][0]
        for side in range(2):
            send_zh[0, side, side, c, cz - 1] = BANDS[c][3]
            send_zh[1, side, side, c, 0] = BANDS[c][0]
    main = scale * np.concatenate([own, send_z.reshape(2 * fy, rows)], 0)
    fill = np.zeros((12, 4 * cz))
    small = scale * np.concatenate([halo[inner:], send_zh.reshape(4, 4 * cz), fill], 0)
    back = np.zeros((fy * fz, fy * fz))
    for at, (z, y) in enumerate(order):
        back[at, y * fz + z] = 1.0
    return [t.astype(jnp.bfloat16) for t in (main, small, back)]


def rowsum(prod):
    width = prod.shape[1] // 2
    half = prod[:, :width] + prod[:, width:]
    return jnp.sum(half.T, axis=0, keepdims=True)


def make_kernel(cx, cy, cz, slots, scale):
    fx, fy, fz = 2 * cx, 2 * cy, 2 * cz
    face = cy * cz
    cells = fy * fz
    rows = 4 * face
    inv = 1.0 / (scale * scale)
    _, inner, y_rows, z_rows = cell_order(fy, fz)
    edge = y_rows + z_rows

    def kernel(coef, cnt, off, ktile, main_h, small_h, back_h, den,
               cv, ax, main, small, back, xo, xi, yo, yi, zo, zi, zrow, zco, zci, phis, edges, den_in, den_ed,
               tiles, tile, lsem, ssem, rsem):
        ix, iy, iz = lax.axis_index("gx"), lax.axis_index("gy"), lax.axis_index("gz")
        gx, gy, gz = lax.axis_size("gx"), lax.axis_size("gy"), lax.axis_size("gz")
        index = {"gx": ix, "gy": iy, "gz": iz}
        size = {"gx": gx, "gy": gy, "gz": gz}

        def local(i, src, dst):
            return pltpu.make_async_copy(src, dst, lsem.at[i])

        loads = [
            local(0, coef.at[:, 0], cv.at[:, 0]),
            local(1, coef.at[:, cx - 1], cv.at[:, cx - 1]),
            local(2, coef.at[:, pl.ds(1, cx - 2)], cv.at[:, pl.ds(1, cx - 2)]),
            local(3, main_h, main),
            local(4, small_h, small),
            local(5, ktile.at[0], tiles.at[2]),
            local(6, back_h, back),
        ]
        for load in loads:
            load.start()

        def has(axis, step):
            return index[axis] < size[axis] - 1 if step > 0 else index[axis] > 0

        barrier = pltpu.get_barrier_semaphore()
        ring = {1: lax.rem(ix + 1, gx), -1: lax.rem(ix + gx - 1, gx)}
        for step in (1, -1):
            pl.semaphore_signal(barrier, inc=1, device_id={"gx": ring[step]}, device_id_type=MESH)
            for axis in ("gy", "gz"):
                @pl.when(has(axis, step))
                def _():
                    pl.semaphore_signal(
                        barrier, inc=1, device_id={axis: index[axis] + step}, device_id_type=MESH
                    )

        def remote(i, src, dst, axis, target):
            return pltpu.make_async_remote_copy(
                src_ref=src, dst_ref=dst, send_sem=ssem.at[i], recv_sem=rsem.at[i],
                device_id={axis: target}, device_id_type=MESH,
            )

        early, late = pl.ds(2, fx - 2), pl.ds(0, 2)
        up, dn = 0, 1
        copies = {}
        for side, step in ((up, 1), (dn, -1)):
            copies["x", side] = (remote(side, xo.at[side], xi.at[side], "gx", ix + step), "gx", step)
            for part, (name, planes) in enumerate((("e", early), ("l", late))):
                copies["y" + name, side] = (
                    remote(4 + 2 * part + side, yo.at[side, planes],
                           yi.at[planes, pl.ds(side * 2 * cz, 2 * cz)], "gy", iy + step),
                    "gy", step)
                copies["z" + name, side] = (
                    remote(8 + 2 * part + side, zo.at[side, planes], zi.at[side, planes], "gz", iz + step),
                    "gz", step)
            copies["zc", side] = (remote(14 + side, zco.at[side], zci.at[side], "gz", iz + step), "gz", step)
        core = iy % 2
        part = pl.ds(core * (slots // 2), slots // 2)
        rings = [remote(2 + side, ktile.at[0, part], tiles.at[side, part], "gx", ring[step])
                 for side, step in ((up, 1), (dn, -1))]
        passes = [remote(12 + side, tiles.at[side, part], tiles.at[side, part], "gy", iy + 1 - 2 * core)
                  for side in (up, dn)]

        def start(key):
            copy, axis, step = copies[key]
            pl.when(has(axis, step))(lambda: copy.start())

        def arrive(key):
            copy, axis, step = copies[key]
            pl.when(has(axis, -step))(lambda: copy.wait_recv())

        @pl.when(ix == 0)
        def _():
            xi[0] = jnp.zeros(xi.shape[1:], BF)

        @pl.when(ix == gx - 1)
        def _():
            xi[1] = jnp.zeros(xi.shape[1:], BF)

        @pl.when(iy == 0)
        def _():
            yi[:, 0 : 2 * cz] = jnp.zeros((fx, 2 * cz, slots), BF)

        @pl.when(iy == gy - 1)
        def _():
            yi[:, 2 * cz : 4 * cz] = jnp.zeros((fx, 2 * cz, slots), BF)

        @pl.when(iz == 0)
        def _():
            zi[0] = jnp.zeros(zi.shape[1:], BF)
            zci[0] = jnp.zeros(zci.shape[1:], BF)

        @pl.when(iz == gz - 1)
        def _():
            zi[1] = jnp.zeros(zi.shape[1:], BF)
            zci[1] = jnp.zeros(zci.shape[1:], BF)

        live = jnp.where(
            lax.broadcasted_iota(jnp.int32, (1, slots), 1) < cnt[0, 0, 0], 1.0, 0.0
        ).astype(F32)
        low = [FILT[t] * live for t in range(4)]
        high = [WAVE[t] * live for t in range(4)]

        def bands(k, p):
            return cv[p, k].astype(F32), cv[4 + p, k].astype(F32)

        def block(p):
            return pl.ds(p * face, face)

        loads[0].wait()
        for p in range(4):
            s, w = bands(0, p)
            xo[dn, block(p)] = (low[0] * s + high[0] * w).astype(BF)
        loads[1].wait()
        for p in range(4):
            s, w = bands(cx - 1, p)
            xo[up, block(p)] = (low[3] * s + high[3] * w).astype(BF)
        peers = 2
        for axis in ("gy", "gz"):
            i, n = index[axis], size[axis]
            peers = peers + (i + n - 1) // n + ((i + 1) % n + n - 1) // n
        pl.semaphore_wait(barrier, peers)
        start(("x", dn))
        start(("x", up))

        loads[2].wait()

        def send_y(q):
            for side, tap, k in ((up, 3, cy - 1), (dn, 0, 0)):
                parts = []
                for c in range(2):
                    s = ax[q, pl.ds(c * face + k * cz, cz)].astype(F32)
                    w = ax[q, pl.ds((2 + c) * face + k * cz, cz)].astype(F32)
                    parts.append(FILT[tap] * s + WAVE[tap] * w)
                yo[side, q] = jnp.concatenate(parts, axis=0).astype(BF)

        @pl.loop(1, cx)
        def _(m):
            for p in range(4):
                s0, w0 = bands(m - 1, p)
                s1, w1 = bands(m, p)
                ax[2 * m, block(p)] = (
                    low[2] * s0 + high[2] * w0 + low[0] * s1 + high[0] * w1
                ).astype(BF)
                ax[2 * m + 1, block(p)] = (
                    low[1] * s1 + high[1] * w1 + low[3] * s0 + high[3] * w0
                ).astype(BF)
            send_y(2 * m)
            send_y(2 * m + 1)

        start(("ye", up))
        start(("ye", dn))
        for copy in rings:
            copy.start()
        loads[3].wait()
        loads[4].wait()

        def own_cells(q):
            pre = jnp.dot(main[...], ax[q], preferred_element_type=F32)
            phis[q] = pre[:inner].astype(BF)
            edges[q] = pre[inner : cells]
            zo[up, q] = pre[cells : cells + fy].astype(BF)
            zo[dn, q] = pre[cells + fy :].astype(BF)

        for q in range(2, fx):
            own_cells(q)
        start(("ze", up))
        start(("ze", dn))

        arrive(("x", up))
        arrive(("x", dn))
        for p in range(4):
            s, w = bands(cx - 1, p)
            ax[0, block(p)] = (low[2] * s + high[2] * w + xi[dn, block(p)].astype(F32)).astype(BF)
            s, w = bands(0, p)
            ax[1, block(p)] = (low[1] * s + high[1] * w + xi[up, block(p)].astype(F32)).astype(BF)
        send_y(0)
        send_y(1)
        start(("yl", up))
        start(("yl", dn))

        own_cells(0)
        own_cells(1)
        start(("zl", up))
        start(("zl", dn))

        def y_halo(q):
            add = jnp.dot(small[...], yi[q], preferred_element_type=F32)
            edges[q] = edges[q] + add[:edge]
            for row in range(4):
                zrow[row // 2, pl.ds(row % 2 * fx + q, 1), :] = add[edge + row : edge + row + 1]

        arrive(("ye", up))
        arrive(("ye", dn))
        for q in range(2, fx):
            y_halo(q)
        arrive(("yl", up))
        arrive(("yl", dn))
        y_halo(0)
        y_halo(1)
        zco[...] = zrow[...].astype(BF)
        start(("zc", up))
        start(("zc", dn))

        for copy, onward in zip(rings, passes):
            copy.wait_recv()
            onward.start()
        loads[5].wait()
        loads[6].wait()
        for copy in passes:
            copy.wait_recv()
        away = off[0, 0, 0]
        before = jnp.where(away == -1, 1.0, 0.0).astype(F32)
        after = jnp.where(away == 1, 1.0, 0.0).astype(F32)
        here = 1.0 - before - after
        tile[...] = (
            tiles[up].astype(F32) * before + tiles[dn].astype(F32) * after
            + tiles[2].astype(F32) * here
        ).astype(BF)

        def dens(phi):
            psi = jnp.dot(phi, tile[...], preferred_element_type=F32)
            return rowsum(phi.astype(F32) * psi) * inv

        for q in range(fx):
            den_in[pl.ds((q - 1) % fx, 1), :] = dens(phis[q])

        def edge_cells(pre, at, width):
            row = dens(pre.reshape(fx * width, slots).astype(BF))
            for q in range(fx):
                den_ed[pl.ds((q - 1) % fx, 1), pl.ds(at, width)] = row[:, q * width : (q + 1) * width]

        def restore(value, at):
            return jnp.dot(value, back[pl.ds(at, value.shape[1]), :].astype(F32),
                           precision=lax.Precision.HIGHEST, preferred_element_type=F32)

        edge_cells(edges[:, :y_rows], 0, y_rows)
        placed = restore(den_in[...], 0)
        for key in ("ze", "zl", "zc"):
            arrive((key, up))
            arrive((key, dn))
        y_at = lax.broadcasted_iota(jnp.int32, (fx, fy, slots), 1)

        def z_face(side):
            late_rows = zci[side].astype(F32)
            pre = edges[:, y_rows + side * fy : y_rows + (side + 1) * fy] + zi[side].astype(F32)
            pre += jnp.where(y_at == 0, late_rows[:fx, None, :], 0.0)
            return pre + jnp.where(y_at == fy - 1, late_rows[fx:, None, :], 0.0)

        pre = jnp.concatenate([z_face(0), z_face(1)], axis=1)
        edge_cells(pre, y_rows, z_rows)
        den[...] = placed + restore(den_ed[...], inner)

        for copy, axis, step in copies.values():
            pl.when(has(axis, step))(lambda copy=copy: copy.wait_send())
        for copy in rings + passes:
            copy.wait_send()

    return kernel


def body(coefficients, fun_count, tile_offset, kernel):
    bands, cx, cy, cz, slots = coefficients.shape
    fx, fy, fz = 2 * cx, 2 * cy, 2 * cz
    cells, rows = fy * fz, 4 * cy * cz
    scale = best_scale()
    main, small, back = tables(cy, cz, scale)
    _, inner, y_rows, z_rows = cell_order(fy, fz)
    anywhere = pl.BlockSpec(memory_space=pltpu.HBM)
    scalar = pl.BlockSpec(memory_space=pltpu.SMEM)
    vmem = pl.BlockSpec(memory_space=pltpu.VMEM)
    den = pl.pallas_call(
        make_kernel(cx, cy, cz, slots, scale),
        out_shape=jax.ShapeDtypeStruct((fx, cells), F32),
        in_specs=[anywhere, scalar, scalar, anywhere, anywhere, anywhere, anywhere],
        out_specs=vmem,
        scratch_shapes=[
            pltpu.VMEM((bands, cx, cy * cz, slots), BF),
            pltpu.VMEM((fx, rows, slots), BF),
            pltpu.VMEM(main.shape, BF),
            pltpu.VMEM(small.shape, BF),
            pltpu.VMEM(back.shape, BF),
            pltpu.VMEM((2, rows, slots), BF),
            pltpu.VMEM((2, rows, slots), BF),
            pltpu.VMEM((2, fx, 2 * cz, slots), BF),
            pltpu.VMEM((fx, 4 * cz, slots), BF),
            pltpu.VMEM((2, fx, fy, slots), BF),
            pltpu.VMEM((2, fx, fy, slots), BF),
            pltpu.VMEM((2, 2 * fx, slots), F32),
            pltpu.VMEM((2, 2 * fx, slots), BF),
            pltpu.VMEM((2, 2 * fx, slots), BF),
            pltpu.VMEM((fx, inner, slots), BF),
            pltpu.VMEM((fx, y_rows + z_rows, slots), F32),
            pltpu.VMEM((fx, inner), F32),
            pltpu.VMEM((fx, y_rows + z_rows), F32),
            pltpu.VMEM((3, slots, slots), BF),
            pltpu.VMEM((slots, slots), BF),
            pltpu.SemaphoreType.DMA((7,)),
            pltpu.SemaphoreType.DMA((16,)),
            pltpu.SemaphoreType.DMA((16,)),
        ],
        compiler_params=pltpu.CompilerParams(
            collective_id=0, has_side_effects=True, vmem_limit_bytes=63 * 2**20
        ),
    )(
        coefficients.reshape(bands, cx, cy * cz, slots),
        fun_count, tile_offset, kernel, jnp.asarray(main), jnp.asarray(small),
        jnp.asarray(back),
    )
    return den.reshape(1, 1, 1, -1)


def solution(mesh):
    placed = (
        P(None, "gx", "gy", "gz", None),
        P("gx", "gy", "gz"),
        P("gx", "gy", "gz"),
        P("gx", None, None),
    )
    return jax.shard_map(
        body, mesh=mesh, in_specs=placed, out_specs=P("gx", "gy", "gz", None), check_vma=False
    )
```

```python
import jax
import jax.numpy as jnp
import numpy as np
from jax import lax
from jax.experimental import pallas as pl
from jax.experimental.pallas import tpu as pltpu
from jax.sharding import PartitionSpec as P

FILT = [0.48296291314453416, 0.8365163037378079, 0.2241438680420134, -0.12940952255126037]
WAVE = [(1.0 if t % 2 == 0 else -1.0) * FILT[3 - t] for t in range(4)]
BANDS = (FILT, WAVE)
MESH = pl.DeviceIdType.MESH
BF = jnp.bfloat16
F32 = jnp.float32


def synthesis(coarse):
    table = np.zeros((2 * coarse, 2, coarse))
    for n in range(2 * coarse):
        for k in range(coarse):
            t = n - 2 * k + 1
            if 0 <= t < 4:
                for b in range(2):
                    table[n, b, k] = BANDS[b][t]
    return table


def best_scale():
    taps = np.array(FILT)
    prods = (taps[:, None] * taps[None, :]).reshape(-1)
    scales = np.linspace(1.0, 2.0, 4001)
    scaled = scales[:, None] * prods[None, :]
    rounded = scaled.astype(jnp.bfloat16).astype(np.float64)
    errors = np.sum(((rounded - scaled) / scales[:, None]) ** 2, axis=1)
    return float(scales[int(np.argmin(errors))])


def cell_order(fy, fz):
    z_faces = [(z, y) for z in (0, fz - 1) for y in range(fy)]
    y_faces = [(z, y) for y in (0, fy - 1) for z in range(1, fz - 1)]
    inner = [(z, y) for z in range(1, fz - 1) for y in range(1, fy - 1)]
    fill = -len(y_faces) % 16
    y_faces, inner = y_faces + inner[:fill], inner[fill:]
    return inner + y_faces + z_faces, len(inner), len(y_faces), len(z_faces)


def tables(cy, cz, scale):
    sy, sz = synthesis(cy), synthesis(cz)
    fy, fz = 2 * cy, 2 * cz
    rows = 4 * cy * cz
    order, inner, y_rows, z_rows = cell_order(fy, fz)
    pick = np.array([z * fy + y for z, y in order])
    own = np.einsum("ybk,zcl->zybckl", sy, sz).reshape(fy * fz, rows)[pick]
    halo = np.zeros((fz, fy, 2, 2, cz))
    halo[:, 0, 0] = sz
    halo[:, fy - 1, 1] = sz
    halo = halo.reshape(fy * fz, 4 * cz)[pick]
    send_z = np.zeros((2, fy, 2, 2, cy, cz))
    send_zh = np.zeros((2, 2, 2, 2, cz))
    for c in range(2):
        for b in range(2):
            send_z[0, :, b, c, :, cz - 1] = sy[:, b] * BANDS[c][3]
            send_z[1, :, b, c, :, 0] = sy[:, b] * BANDS[c][0]
        for side in range(2):
            send_zh[0, side, side, c, cz - 1] = BANDS[c][3]
            send_zh[1, side, side, c, 0] = BANDS[c][0]
    main = scale * np.concatenate([own, send_z.reshape(2 * fy, rows)], 0)
    fill = np.zeros((12, 4 * cz))
    small = scale * np.concatenate([halo[inner:], send_zh.reshape(4, 4 * cz), fill], 0)
    back = np.zeros((fy * fz, fy * fz))
    for at, (z, y) in enumerate(order):
        back[at, y * fz + z] = 1.0
    return [t.astype(jnp.bfloat16) for t in (main, small, back)]


def rowsum(prod):
    width = prod.shape[1] // 2
    half = prod[:, :width] + prod[:, width:]
    return jnp.sum(half.T, axis=0, keepdims=True)


def make_kernel(cx, cy, cz, slots, scale):
    fx, fy, fz = 2 * cx, 2 * cy, 2 * cz
    face = cy * cz
    cells = fy * fz
    rows = 4 * face
    inv = 1.0 / (scale * scale)
    _, inner, y_rows, z_rows = cell_order(fy, fz)
    edge = y_rows + z_rows

    def kernel(coef, cnt, off, ktile, main_h, small_h, back_h, den,
               cv, ax, main, small, back, xo, xi, yo, yi, zo, zi, zrow, zco, zci, phis, edges, den_in, den_ed,
               tiles, tile, lsem, ssem, rsem):
        ix, iy, iz = lax.axis_index("gx"), lax.axis_index("gy"), lax.axis_index("gz")
        gx, gy, gz = lax.axis_size("gx"), lax.axis_size("gy"), lax.axis_size("gz")
        index = {"gx": ix, "gy": iy, "gz": iz}
        size = {"gx": gx, "gy": gy, "gz": gz}

        def local(i, src, dst):
            return pltpu.make_async_copy(src, dst, lsem.at[i])

        loads = [
            local(0, coef.at[:, 0], cv.at[:, 0]),
            local(1, coef.at[:, cx - 1], cv.at[:, cx - 1]),
            local(2, coef.at[:, pl.ds(1, cx - 2)], cv.at[:, pl.ds(1, cx - 2)]),
            local(3, main_h, main),
            local(4, small_h, small),
            local(5, ktile.at[0], tiles.at[2]),
            local(6, back_h, back),
        ]
        for load in loads:
            load.start()

        def has(axis, step):
            return index[axis] < size[axis] - 1 if step > 0 else index[axis] > 0

        barrier = pltpu.get_barrier_semaphore()
        ring = {1: lax.rem(ix + 1, gx), -1: lax.rem(ix + gx - 1, gx)}
        for step in (1, -1):
            pl.semaphore_signal(barrier, inc=1, device_id={"gx": ring[step]}, device_id_type=MESH)
            for axis in ("gy", "gz"):
                @pl.when(has(axis, step))
                def _():
                    pl.semaphore_signal(
                        barrier, inc=1, device_id={axis: index[axis] + step}, device_id_type=MESH
                    )

        def remote(i, src, dst, axis, target):
            return pltpu.make_async_remote_copy(
                src_ref=src, dst_ref=dst, send_sem=ssem.at[i], recv_sem=rsem.at[i],
                device_id={axis: target}, device_id_type=MESH,
            )

        early, late = pl.ds(2, fx - 2), pl.ds(0, 2)
        up, dn = 0, 1
        copies = {}
        for side, step in ((up, 1), (dn, -1)):
            copies["x", side] = (remote(side, xo.at[side], xi.at[side], "gx", ix + step), "gx", step)
            for part, (name, planes) in enumerate((("e", early), ("l", late))):
                copies["y" + name, side] = (
                    remote(4 + 2 * part + side, yo.at[side, planes],
                           yi.at[planes, pl.ds(side * 2 * cz, 2 * cz)], "gy", iy + step),
                    "gy", step)
                copies["z" + name, side] = (
                    remote(8 + 2 * part + side, zo.at[side, planes], zi.at[side, planes], "gz", iz + step),
                    "gz", step)
            copies["zc", side] = (remote(14 + side, zco.at[side], zci.at[side], "gz", iz + step), "gz", step)
        core = iy % 2
        part = pl.ds(core * (slots // 2), slots // 2)
        rings = [remote(2 + side, ktile.at[0, part], tiles.at[side, part], "gx", ring[step])
                 for side, step in ((up, 1), (dn, -1))]
        passes = [remote(12 + side, tiles.at[side, part], tiles.at[side, part], "gy", iy + 1 - 2 * core)
                  for side in (up, dn)]

        def start(key):
            copy, axis, step = copies[key]
            pl.when(has(axis, step))(lambda: copy.start())

        def arrive(key):
            copy, axis, step = copies[key]
            pl.when(has(axis, -step))(lambda: copy.wait_recv())

        @pl.when(ix == 0)
        def _():
            xi[0] = jnp.zeros(xi.shape[1:], BF)

        @pl.when(ix == gx - 1)
        def _():
            xi[1] = jnp.zeros(xi.shape[1:], BF)

        @pl.when(iy == 0)
        def _():
            yi[:, 0 : 2 * cz] = jnp.zeros((fx, 2 * cz, slots), BF)

        @pl.when(iy == gy - 1)
        def _():
            yi[:, 2 * cz : 4 * cz] = jnp.zeros((fx, 2 * cz, slots), BF)

        @pl.when(iz == 0)
        def _():
            zi[0] = jnp.zeros(zi.shape[1:], BF)
            zci[0] = jnp.zeros(zci.shape[1:], BF)

        @pl.when(iz == gz - 1)
        def _():
            zi[1] = jnp.zeros(zi.shape[1:], BF)
            zci[1] = jnp.zeros(zci.shape[1:], BF)

        live = jnp.where(
            lax.broadcasted_iota(jnp.int32, (1, slots), 1) < cnt[0, 0, 0], 1.0, 0.0
        ).astype(F32)
        low = [FILT[t] * live for t in range(4)]
        high = [WAVE[t] * live for t in range(4)]

        def bands(k, p):
            return cv[p, k].astype(F32), cv[4 + p, k].astype(F32)

        def block(p):
            return pl.ds(p * face, face)

        loads[0].wait()
        for p in range(4):
            s, w = bands(0, p)
            xo[dn, block(p)] = (low[0] * s + high[0] * w).astype(BF)
        loads[1].wait()
        for p in range(4):
            s, w = bands(cx - 1, p)
            xo[up, block(p)] = (low[3] * s + high[3] * w).astype(BF)
        peers = 2
        for axis in ("gy", "gz"):
            i, n = index[axis], size[axis]
            peers = peers + (i + n - 1) // n + ((i + 1) % n + n - 1) // n
        pl.semaphore_wait(barrier, peers)
        start(("x", dn))
        start(("x", up))

        loads[2].wait()

        def send_y(q):
            for side, tap, k in ((up, 3, cy - 1), (dn, 0, 0)):
                parts = []
                for c in range(2):
                    s = ax[q, pl.ds(c * face + k * cz, cz)].astype(F32)
                    w = ax[q, pl.ds((2 + c) * face + k * cz, cz)].astype(F32)
                    parts.append(FILT[tap] * s + WAVE[tap] * w)
                yo[side, q] = jnp.concatenate(parts, axis=0).astype(BF)

        @pl.loop(1, cx)
        def _(m):
            for p in range(4):
                s0, w0 = bands(m - 1, p)
                s1, w1 = bands(m, p)
                ax[2 * m, block(p)] = (
                    low[2] * s0 + high[2] * w0 + low[0] * s1 + high[0] * w1
                ).astype(BF)
                ax[2 * m + 1, block(p)] = (
                    low[1] * s1 + high[1] * w1 + low[3] * s0 + high[3] * w0
                ).astype(BF)
            send_y(2 * m)
            send_y(2 * m + 1)

        start(("ye", up))
        start(("ye", dn))
        for copy in rings:
            copy.start()
        loads[3].wait()
        loads[4].wait()

        def own_cells(q):
            pre = jnp.dot(main[...], ax[q], preferred_element_type=F32)
            phis[q] = pre[:inner].astype(BF)
            edges[q] = pre[inner : cells]
            zo[up, q] = pre[cells : cells + fy].astype(BF)
            zo[dn, q] = pre[cells + fy :].astype(BF)

        for q in range(2, fx):
            own_cells(q)
        start(("ze", up))
        start(("ze", dn))

        arrive(("x", up))
        arrive(("x", dn))
        for p in range(4):
            s, w = bands(cx - 1, p)
            ax[0, block(p)] = (low[2] * s + high[2] * w + xi[dn, block(p)].astype(F32)).astype(BF)
            s, w = bands(0, p)
            ax[1, block(p)] = (low[1] * s + high[1] * w + xi[up, block(p)].astype(F32)).astype(BF)
        send_y(0)
        send_y(1)
        start(("yl", up))
        start(("yl", dn))

        own_cells(0)
        own_cells(1)
        start(("zl", up))
        start(("zl", dn))

        def y_halo(q):
            add = jnp.dot(small[...], yi[q], preferred_element_type=F32)
            edges[q] = edges[q] + add[:edge]
            for row in range(4):
                zrow[row // 2, pl.ds(row % 2 * fx + q, 1), :] = add[edge + row : edge + row + 1]

        arrive(("ye", up))
        arrive(("ye", dn))
        for q in range(2, fx):
            y_halo(q)
        arrive(("yl", up))
        arrive(("yl", dn))
        y_halo(0)
        y_halo(1)
        zco[...] = zrow[...].astype(BF)
        start(("zc", up))
        start(("zc", dn))

        for copy, onward in zip(rings, passes):
            copy.wait_recv()
            onward.start()
        loads[5].wait()
        loads[6].wait()
        for copy in passes:
            copy.wait_recv()
        away = off[0, 0, 0]
        before = jnp.where(away == -1, 1.0, 0.0).astype(F32)
        after = jnp.where(away == 1, 1.0, 0.0).astype(F32)
        here = 1.0 - before - after
        tile[...] = (
            tiles[up].astype(F32) * before + tiles[dn].astype(F32) * after
            + tiles[2].astype(F32) * here
        ).astype(BF)

        def dens(phi):
            psi = jnp.dot(phi, tile[...], preferred_element_type=F32)
            return rowsum(phi.astype(F32) * psi) * inv

        for q in range(fx):
            den_in[pl.ds((q - 1) % fx, 1), :] = dens(phis[q])

        def edge_cells(pre, at, width):
            row = dens(pre.reshape(fx * width, slots).astype(BF))
            for q in range(fx):
                den_ed[pl.ds((q - 1) % fx, 1), pl.ds(at, width)] = row[:, q * width : (q + 1) * width]

        def restore(value, at):
            return jnp.dot(value, back[pl.ds(at, value.shape[1]), :].astype(F32),
                           precision=lax.Precision.HIGHEST, preferred_element_type=F32)

        edge_cells(edges[:, :y_rows], 0, y_rows)
        placed = restore(den_in[...], 0)
        for key in ("ze", "zl", "zc"):
            arrive((key, up))
            arrive((key, dn))
        y_at = lax.broadcasted_iota(jnp.int32, (fx, fy, slots), 1)

        def z_face(side):
            late_rows = zci[side].astype(F32)
            pre = edges[:, y_rows + side * fy : y_rows + (side + 1) * fy] + zi[side].astype(F32)
            pre += jnp.where(y_at == 0, late_rows[:fx, None, :], 0.0)
            return pre + jnp.where(y_at == fy - 1, late_rows[fx:, None, :], 0.0)

        pre = jnp.concatenate([z_face(0), z_face(1)], axis=1)
        edge_cells(pre, y_rows, z_rows)
        flat = placed + restore(den_ed[...], inner)
        for n in range(fx):
            den[:, pl.ds(n * cells, cells)] = flat[n : n + 1]

        for copy, axis, step in copies.values():
            pl.when(has(axis, step))(lambda copy=copy: copy.wait_send())
        for copy in rings + passes:
            copy.wait_send()

    return kernel


def body(coefficients, fun_count, tile_offset, kernel):
    bands, cx, cy, cz, slots = coefficients.shape
    fx, fy, fz = 2 * cx, 2 * cy, 2 * cz
    cells, rows = fy * fz, 4 * cy * cz
    scale = best_scale()
    main, small, back = tables(cy, cz, scale)
    _, inner, y_rows, z_rows = cell_order(fy, fz)
    anywhere = pl.BlockSpec(memory_space=pltpu.HBM)
    scalar = pl.BlockSpec(memory_space=pltpu.SMEM)
    vmem = pl.BlockSpec(memory_space=pltpu.VMEM)
    den = pl.pallas_call(
        make_kernel(cx, cy, cz, slots, scale),
        out_shape=jax.ShapeDtypeStruct((1, fx * cells), F32),
        in_specs=[anywhere, scalar, scalar, anywhere, anywhere, anywhere, anywhere],
        out_specs=vmem,
        scratch_shapes=[
            pltpu.VMEM((bands, cx, cy * cz, slots), BF),
            pltpu.VMEM((fx, rows, slots), BF),
            pltpu.VMEM(main.shape, BF),
            pltpu.VMEM(small.shape, BF),
            pltpu.VMEM(back.shape, BF),
            pltpu.VMEM((2, rows, slots), BF),
            pltpu.VMEM((2, rows, slots), BF),
            pltpu.VMEM((2, fx, 2 * cz, slots), BF),
            pltpu.VMEM((fx, 4 * cz, slots), BF),
            pltpu.VMEM((2, fx, fy, slots), BF),
            pltpu.VMEM((2, fx, fy, slots), BF),
            pltpu.VMEM((2, 2 * fx, slots), F32),
            pltpu.VMEM((2, 2 * fx, slots), BF),
            pltpu.VMEM((2, 2 * fx, slots), BF),
            pltpu.VMEM((fx, inner, slots), BF),
            pltpu.VMEM((fx, y_rows + z_rows, slots), F32),
            pltpu.VMEM((fx, inner), F32),
            pltpu.VMEM((fx, y_rows + z_rows), F32),
            pltpu.VMEM((3, slots, slots), BF),
            pltpu.VMEM((slots, slots), BF),
            pltpu.SemaphoreType.DMA((7,)),
            pltpu.SemaphoreType.DMA((16,)),
            pltpu.SemaphoreType.DMA((16,)),
        ],
        compiler_params=pltpu.CompilerParams(
            collective_id=0, has_side_effects=True, vmem_limit_bytes=63 * 2**20
        ),
    )(
        coefficients.reshape(bands, cx, cy * cz, slots),
        fun_count, tile_offset, kernel, jnp.asarray(main), jnp.asarray(small),
        jnp.asarray(back),
    )
    return den.reshape(1, 1, 1, -1)


def solution(mesh):
    placed = (
        P(None, "gx", "gy", "gz", None),
        P("gx", "gy", "gz"),
        P("gx", "gy", "gz"),
        P("gx", None, None),
    )
    return jax.shard_map(
        body, mesh=mesh, in_specs=placed, out_specs=P("gx", "gy", "gz", None), check_vma=False
    )
```
